256 devices in a mesh: dp: 64 (over z, x, core), tensor: 4 (over y).
Axes of the slice: x: 4, y: 4, z: 8, core: 2. Of those that a mesh axis runs over, the one named last changes fastest.
Arguments:
- hidden: bfloat16 [4096, 8, 3, 5120], P('dp', None, None, 'tensor'), may hold values from -6 to 6
- assign: int32 [4096], P('dp'), may hold values from 0 to 63, as said below
- query: bfloat16 [4096, 8, 2560], P('dp', None, 'tensor'), may hold values from -36 to 36
- d_out: bfloat16 [4096, 8, 2560], P('dp', None, 'tensor'), may hold values from -6 to 6
- doc_ids: int32 [4096, 8], P('dp'), may hold values from 0 to 2, never falling along the last dimension, each value on 1 to 4 neighbouring positions
- seq_len: int32 [4096], P('dp'), may hold values from 1 to 8
- w_kv: bfloat16 [1024, 3, 5120], P('dp', None, 'tensor'), may hold values from -1.25 to 1.25
Outputs:
- attn_out: bfloat16 [4096, 8, 2560], P('dp', None, 'tensor')
- grad_w: float32 [1024, 3, 5120], P('dp', None, 'tensor')
The draws below stay inside these ranges and needn't reach their ends.
Inputs may be any that keep to these rules, and one draw needn't show every extreme that they name: Within each aligned block of 64 entries, assign is a permutation of 0 to 63.
All inputs are finite; a program needn't handle non-finite values.
Results may differ from the reference program's by a relative error of at most 0.009.
The reference program's roundings to bfloat16 on the way count: a program that leaves them out, or rounds other values in their place, can miss the bound.
Values may be sent and summed in bfloat16 or wider, within the bound.
No kernel may reach another device: no remote copies, remote signals or barrier semaphores. Data moves between devices by JAX's collectives and lax.ppermute only.
A program may use at most 128 MiB of HBM per device.

```python
import math
import jax
import jax.numpy as jnp
import numpy as np

D = 5120
HD = 128
QH = 20
KVH = 4
SEQ = 8
SEQS_DEV = 64
SEQS = 4096
COLS = 1024
N_DP = 64


def draw_hidden(key, part):
    own_key = jax.random.fold_in(key, 11)
    shape = (SEQS, SEQ, 3, D)
    values = jnp.clip(jax.random.normal(own_key, shape, jnp.float32), -6.0, 6.0)
    return values.astype(jnp.bfloat16)


def draw_w_kv(key, part):
    own_key = jax.random.fold_in(key, 13)
    values = jnp.clip(jax.random.normal(own_key, (COLS, 3, D), jnp.float32), -6.0, 6.0) * (3 * D) ** (-0.5)
    return values.astype(jnp.bfloat16)


def draw_query(key, part):
    own_key = jax.random.fold_in(key, 17)
    shape = (SEQS, SEQ, QH * HD)
    base = jnp.clip(jax.random.normal(own_key, shape, jnp.float32), -6.0, 6.0)
    values = base
    return values.astype(jnp.bfloat16)


def draw_assign(key, part):
    subkeys = jax.random.split(key, SEQS // SEQS_DEV)

    def shuffle(subkey):
        return jax.random.permutation(subkey, SEQS_DEV)
    shuffled = jax.vmap(shuffle)(subkeys)
    return shuffled.reshape(-1).astype(jnp.int32)


def draw_seq_len(key, part):
    lengths = jax.random.randint(key, (SEQS,), 1, SEQ + 1)
    lengths = lengths.at[0].set(SEQ)
    lengths = lengths.at[1].set(1)
    return lengths.astype(jnp.int32)


def level_of(key, extent, pieces, smallest, top_value):
    factor_of, own = 1.0, jax.random.fold_in(key, 6)
    for position, blocks in pieces:
        heights = jnp.exp(jax.random.uniform(jax.random.fold_in(own, position), (blocks,), jnp.float32, smallest / len(pieces), top_value / len(pieces)))
        factor_of = factor_of * jnp.repeat(heights, extent[position] // blocks).reshape([-1 if axis == position else 1 for axis in range(len(extent))])
    return factor_of


def profile(amount, total, most, lean):
    loads = [(1 << 20) // math.isqrt(rank ** lean) + 1 for rank in range(2, amount + 1)]
    spare, given = total - most - (amount - 1), [1] * (amount - 1)
    while spare > 0:
        candidates = [i for i in range(amount - 1) if given[i] < most]
        pool, left = sum([loads[i] for i in candidates]), spare
        for i in candidates:
            more = min(most - given[i], max(1, left * loads[i] // pool), spare)
            given[i] = given[i] + more
            spare = spare - more
    return np.array([most] + given)


def ragged_sizes(key, amount, total, most, lean):
    if amount == 2:
        one = jax.random.randint(key, (), max(1, total - most), min(most, total - 1) + 1)
        return jnp.stack([one, total - one])
    sizes = jnp.asarray(profile(amount, total, most, lean), jnp.int32)
    twos = (amount - 1) // 2
    donor, receiver = sizes[1:1 + 2 * twos:2], sizes[2:2 + 2 * twos:2]
    room = jnp.minimum(donor - 1, most - receiver)
    moved = jax.random.randint(jax.random.fold_in(key, 1), (twos,), 0, 1 << 20) % (room + 1)
    sizes = sizes.at[1:1 + 2 * twos:2].set(donor - moved).at[2:2 + 2 * twos:2].set(receiver + moved)
    return sizes[jax.random.permutation(jax.random.fold_in(key, 2), amount)]


def noise(rng, extent, deviation, bound, cuts=(), kind=jnp.bfloat16):
    values = jax.random.normal(rng, extent, jnp.float32) * deviation
    if len(cuts) > 0:
        values = level_of(rng, extent, cuts, -0.22, 0.18) * values
    return jnp.clip(values, min=-bound, max=bound).astype(kind)


def setup_inputs(seed: int = 0) -> dict:
    arg_keys = jax.random.split(jax.random.key(seed), 8)
    return {
        "hidden": draw_hidden(jax.random.fold_in(arg_keys[7], 71), 0),
        "assign": draw_assign(jax.random.fold_in(arg_keys[7], 71), 0),
        "query": draw_query(jax.random.fold_in(arg_keys[7], 71), 0),
        "d_out": noise(arg_keys[3], (SEQS, SEQ, QH * HD), 1.0, 6.0, ((0, 64), (2, 4))),
        "doc_ids": jax.vmap(lambda own: jnp.searchsorted(jnp.cumsum(ragged_sizes(own, 3, SEQ, SEQ // 2, 0)), jnp.arange(SEQ), side="right"))(jax.random.split(arg_keys[4], SEQS)).reshape((SEQS, SEQ)).astype(jnp.int32),
        "seq_len": draw_seq_len(jax.random.fold_in(arg_keys[7], 71), 0),
        "w_kv": draw_w_kv(jax.random.fold_in(arg_keys[7], 71), 0),
    }


def rebalance_order(assign):
    per_peer = SEQS_DEV // N_DP
    slot_ids = jnp.arange(SEQS, dtype=jnp.int32)
    sender = slot_ids // SEQS_DEV
    target = ((slot_ids % SEQS_DEV) // per_peer) * SEQS_DEV + sender * per_peer + slot_ids % per_peer
    source = sender * SEQS_DEV + assign.astype(jnp.int32)
    return jnp.zeros((SEQS,), jnp.int32).at[target].set(source)


def attend(query, keyval, doc_ids, seq_len, d_out):
    seq_count, seq_length = doc_ids.shape
    heads_kv = keyval.shape[2]
    group_size = query.shape[2] // (heads_kv * HD)
    head_scale = HD ** -0.5
    grouped = query.reshape(seq_count, seq_length, heads_kv, group_size, HD).astype(jnp.float32)
    key_rows = keyval[:, :, :, 0, :].astype(jnp.float32)
    value_rows = keyval[:, :, :, 1, :].astype(jnp.float32)
    scores = jnp.einsum("sqgrd,skgd->sgrqk", grouped, key_rows) * head_scale
    positions = jnp.arange(seq_length)
    causal = positions[None, :] <= positions[:, None]
    same_doc = doc_ids[:, :, None] == doc_ids[:, None, :]
    allowed = (causal[None] & same_doc)[:, None, None]
    scores = jnp.where(allowed, scores, -jnp.inf)
    row_max = jnp.max(scores, axis=-1, keepdims=True)
    exponent = jnp.exp(scores - row_max)
    attn_probs = exponent / jnp.sum(exponent, axis=-1, keepdims=True)
    probs_bf = attn_probs.astype(jnp.bfloat16)
    live_rows = positions[None, :] < seq_len[:, None]
    mixed_out = jnp.einsum("sgrqk,skgd->sqgrd", probs_bf.astype(jnp.float32), value_rows)
    mixed_out = jnp.where(live_rows[:, :, None, None, None], mixed_out, 0.0)
    mixed_out = mixed_out.astype(jnp.bfloat16).reshape(seq_count, seq_length, -1)
    cotangent = jnp.where(live_rows[:, :, None], d_out, jnp.zeros((), d_out.dtype))
    cotangent = cotangent.reshape(grouped.shape).astype(jnp.float32)
    prob_grad = jnp.einsum("sqgrd,skgd->sgrqk", cotangent, value_rows)
    score_grad = attn_probs * (prob_grad - jnp.sum(attn_probs * prob_grad, axis=-1, keepdims=True))
    score_bf = score_grad.astype(jnp.bfloat16)
    key_grad = jnp.einsum("sgrqk,sqgrd->skgd", score_bf.astype(jnp.float32), grouped) * head_scale
    value_grad = jnp.einsum("sgrqk,sqgrd->skgd", probs_bf.astype(jnp.float32), cotangent)
    gradients = jnp.stack([key_grad, value_grad], axis=3).astype(jnp.bfloat16)
    return mixed_out, gradients


def reference(hidden, assign, query, d_out, doc_ids, seq_len, w_kv):
    ordering = rebalance_order(assign)
    rows = hidden[ordering].reshape(SEQS * SEQ, 3 * D)
    weights = w_kv.reshape(COLS, 3 * D)
    keyval = jnp.dot(rows, weights.T, preferred_element_type=jnp.float32)
    keyval = keyval.astype(jnp.bfloat16).reshape(SEQS, SEQ, KVH, 2, HD)
    mixed_out, gradients = attend(query, keyval, doc_ids, seq_len, d_out)
    flat_grads = gradients.reshape(SEQS * SEQ, COLS)
    grad_weight = jnp.dot(flat_grads.T, rows, preferred_element_type=jnp.float32)
    return mixed_out, grad_weight.reshape(COLS, 3, D)
```

```python
import jax
import jax.numpy as jnp
from jax import lax
from jax.sharding import Mesh, PartitionSpec as P

HD = 128
BF = jnp.bfloat16
F32 = jnp.float32
SIZES = {"z": 8, "x": 4, "c": 2, "y": 4}
DP = ("z", "x", "c")


def shift(value, axis, step):
    count = SIZES[axis]
    return lax.ppermute(value, axis, [(i, (i + step) % count) for i in range(count)])


def place(buffer, piece, *index):
    index = index + (0,) * (buffer.ndim - len(index))
    return lax.dynamic_update_slice(buffer, piece, index)


def pick(stacked, index, dim=0):
    return lax.dynamic_index_in_dim(stacked, index, dim, keepdims=False)


def ring_gather(own, axis):
    count = SIZES[axis]
    me = lax.axis_index(axis)
    half = own.shape[-1] // 2
    pieces = [(own, me)]
    right = left = own
    for step in range(1, count // 2):
        right = shift(right, axis, 1)
        left = shift(left, axis, -1)
        pieces.append((right, (me - step) % count))
        pieces.append((left, (me + step) % count))
    far_a = shift(right[..., :half], axis, 1)
    far_b = shift(left[..., half:], axis, -1)
    pieces.append((jnp.concatenate([far_a, far_b], -1), (me + count // 2) % count))
    return pieces


def ring_sum(chunks, axis):
    count = SIZES[axis]
    me = lax.axis_index(axis)
    far = chunks((me + count // 2) % count)
    half = far.shape[-1] // 2
    right = shift(far[..., :half].astype(BF), axis, 1)
    left = shift(far[..., half:].astype(BF), axis, -1)
    for step in range(count // 2 - 1, 0, -1):
        to_right = chunks((me + step) % count).astype(F32)
        to_left = chunks((me - step) % count).astype(F32)
        if step == count // 2 - 1:
            to_right = jnp.concatenate(
                [to_right[..., :half] + right.astype(F32), to_right[..., half:]], -1
            )
            to_left = jnp.concatenate(
                [to_left[..., :half], to_left[..., half:] + left.astype(F32)], -1
            )
        else:
            to_right = to_right + right.astype(F32)
            to_left = to_left + left.astype(F32)
        right = shift(to_right.astype(BF), axis, 1)
        left = shift(to_left.astype(BF), axis, -1)
    return chunks(me).astype(F32) + right.astype(F32) + left.astype(F32)


def gather_weights(shard):
    width = shard.shape[-1]
    z_rows = jnp.zeros((8, 8, width), BF)
    x_rows = jnp.zeros((4, 8, width), BF)
    for piece, index in ring_gather(shard[:8], "z"):
        z_rows = place(z_rows, piece[None], index)
    for piece, index in ring_gather(shard[8:], "x"):
        x_rows = place(x_rows, piece[None], index)
    weights = jnp.zeros((8, 4, 16, width), BF)
    for piece, index in ring_gather(z_rows, "x"):
        weights = place(weights, piece[:, None], 0, index, 0)
    for piece, index in ring_gather(x_rows, "z"):
        weights = place(weights, piece[None], index, 0, 8)
    return weights


def scatter_grads(grads):
    upper, lower = grads[:, :, :8], grads[:, :, 8:]
    by_x = ring_sum(lambda i: pick(upper, i, 1), "x")
    by_z = ring_sum(lambda i: pick(lower, i, 0), "z")
    own_upper = ring_sum(lambda i: pick(by_x, i), "z")
    own_lower = ring_sum(lambda i: pick(by_z, i), "x")
    return jnp.concatenate([own_upper, own_lower], 0)


def attend(query, keyval, doc_ids, cotangent):
    seq_count, seq_length = doc_ids.shape
    head_scale = HD ** (-0.5)
    heads = query.shape[2] // HD
    query = query.reshape(seq_count, seq_length, heads, HD)
    cotangent = cotangent.reshape(query.shape)
    key_rows = keyval[:, :, :HD]
    value_rows = keyval[:, :, HD:]
    scores = (
        jnp.einsum("sqrd,skd->srqk", query, key_rows, preferred_element_type=F32) * head_scale
    )
    positions = jnp.arange(seq_length)
    causal = positions[None, :] <= positions[:, None]
    same_doc = doc_ids[:, :, None] == doc_ids[:, None, :]
    allowed = (causal[None] & same_doc)[:, None]
    scores = jnp.where(allowed, scores, -jnp.inf)
    row_max = jnp.max(scores, axis=-1, keepdims=True)
    exponent = jnp.exp(scores - row_max)
    attn_probs = exponent / jnp.sum(exponent, axis=-1, keepdims=True)
    probs_bf = attn_probs.astype(BF)
    mixed_out = jnp.einsum("srqk,skd->sqrd", probs_bf, value_rows, preferred_element_type=F32)
    mixed_out = mixed_out.astype(BF).reshape(seq_count, seq_length, -1)
    prob_grad = jnp.einsum("sqrd,skd->srqk", cotangent, value_rows, preferred_element_type=F32)
    score_grad = attn_probs * (prob_grad - jnp.sum(attn_probs * prob_grad, axis=-1, keepdims=True))
    score_bf = score_grad.astype(BF)
    key_grad = (
        jnp.einsum("srqk,sqrd->skd", score_bf, query, preferred_element_type=F32) * head_scale
    )
    value_grad = jnp.einsum("srqk,sqrd->skd", probs_bf, cotangent, preferred_element_type=F32)
    gradients = jnp.concatenate([key_grad, value_grad], axis=-1).astype(BF)
    return mixed_out, gradients


def column_map(core):
    share = lax.broadcasted_iota(jnp.int32, (HD, 2 * HD), 0)
    whole = lax.broadcasted_iota(jnp.int32, (HD, 2 * HD), 1)
    target = (share // 16) * 32 + core * 16 + share % 16
    return (target == whole).astype(BF)


def body(hidden, assign, query, d_out, doc_ids, seq_len, w_kv):
    seqs, length, levels, features = hidden.shape
    width = levels * features
    rows = seqs * length
    core = lax.axis_index("c")
    head = lax.axis_index("y")
    live = (jnp.arange(length)[None, :] < seq_len[:, None])[:, :, None]
    zero = jnp.zeros((), BF)

    with jax.named_scope("gather_w"):
        weights = gather_weights(w_kv.reshape(w_kv.shape[0], width))
    with jax.named_scope("send_queries"):
        docs = jnp.broadcast_to(doc_ids.astype(BF)[:, :, None], (seqs, length, HD))
        payload = jnp.concatenate([query, jnp.where(live, d_out, zero), docs], -1)
        payload = lax.all_to_all(payload, DP, split_axis=0, concat_axis=0, tiled=True)
        span = query.shape[2]
    with jax.named_scope("swap_rows"):
        slots = hidden.at[assign].get(mode="promise_in_bounds").reshape(rows, width)
        both = jnp.concatenate([slots, shift(slots, "c", 1)], 0)
    with jax.named_scope("project"):
        partial = lax.dot_general(
            both, weights.reshape(-1, width), (((1,), (1,)), ((), ())), preferred_element_type=F32
        )
    with jax.named_scope("sum_features"):
        def share(step):
            return lax.dynamic_slice(partial, (0, ((head + step) % 4) * HD), (2 * rows, HD))
        from_left = shift(share(1), "y", 1)
        from_right = shift(share(-1), "y", -1)
        from_far = shift(share(2), "y", 2)
        summed = (share(0) + from_left + from_right + from_far).astype(BF)
    with jax.named_scope("join_columns"):
        own_map, other_map = column_map(core), column_map(1 - core)
        other = shift(summed[rows:], "c", 1)
        keyval = (
            jnp.dot(summed[:rows], own_map, preferred_element_type=F32)
            + jnp.dot(other, other_map, preferred_element_type=F32)
        ).astype(BF)
    with jax.named_scope("attention"):
        mixed_out, gradients = attend(
            payload[:, :, :span],
            keyval.reshape(seqs, length, 2 * HD),
            payload[:, :, 2 * span].astype(jnp.int32),
            payload[:, :, span : 2 * span],
        )
    with jax.named_scope("split_columns"):
        flat = gradients.reshape(rows, 2 * HD)
        split = (((1,), (1,)), ((), ()))
        mine = lax.dot_general(flat, own_map, split, preferred_element_type=F32).astype(BF)
        theirs = lax.dot_general(flat, other_map, split, preferred_element_type=F32).astype(BF)
        mine = jnp.concatenate([mine, shift(theirs, "c", 1)], 0)
    with jax.named_scope("gather_grads"):
        all_grads = jnp.zeros((2 * rows, 4 * HD), BF)
        for piece, step in (
            (mine, 0),
            (shift(mine, "y", 1), -1),
            (shift(mine, "y", -1), 1),
            (shift(mine, "y", 2), 2),
        ):
            all_grads = place(all_grads, piece, 0, ((head + step) % 4) * HD)
    with jax.named_scope("send_output"):
        mixed_out = lax.all_to_all(mixed_out, DP, split_axis=0, concat_axis=0, tiled=True)
        mixed_out = jnp.where(live, mixed_out, zero)
    with jax.named_scope("weight_grads"):
        grads = lax.dot_general(
            all_grads, both, (((0,), (0,)), ((), ())), preferred_element_type=F32
        ).astype(BF)
    with jax.named_scope("scatter_grads"):
        grad_weight = scatter_grads(grads.reshape(8, 4, 16, width))
    return mixed_out, grad_weight.reshape(w_kv.shape)


def solution(mesh):
    fine = Mesh(mesh.devices.reshape(8, 4, 2, 4), ("z", "x", "c", "y"))
    in_specs = (
        P(DP, None, None, "y"),
        P(DP),
        P(DP, None, "y"),
        P(DP, None, "y"),
        P(DP, None),
        P(DP),
        P(DP, None, "y"),
    )
    out_specs = (P(DP, None, "y"), P(DP, None, "y"))
    return jax.shard_map(body, mesh=fine, in_specs=in_specs, out_specs=out_specs, check_vma=False)
```

```python
import jax
import jax.numpy as jnp
from jax import lax
from jax.experimental import pallas as pl
from jax.experimental.pallas import tpu as pltpu
from jax.sharding import Mesh, PartitionSpec as P

HD = 128
BF = jnp.bfloat16
F32 = jnp.float32
SIZES = {"z": 8, "x": 4, "c": 2, "y": 4}
DP = ("z", "x", "c")


def shift(value, axis, step):
    count = SIZES[axis]
    return lax.ppermute(value, axis, [(i, (i + step) % count) for i in range(count)])


def place(buffer, piece, *index):
    index = index + (0,) * (buffer.ndim - len(index))
    return lax.dynamic_update_slice(buffer, piece, index)


def pick(stacked, index, dim=0):
    return lax.dynamic_index_in_dim(stacked, index, dim, keepdims=False)


def after(value, *others):
    return lax.optimization_barrier((value,) + others)[0]


def ring_gather(own, axis, holds):
    count = SIZES[axis]
    me = lax.axis_index(axis)
    half = own.shape[-1] // 2
    pieces = [(own, me)]
    right = left = own
    for step in range(1, count // 2):
        if step in holds:
            right, left, _ = lax.optimization_barrier((right, left, holds[step]))
        right = shift(right, axis, 1)
        left = shift(left, axis, -1)
        pieces.append((right, (me - step) % count))
        pieces.append((left, (me + step) % count))
    if count // 2 in holds:
        right, left, _ = lax.optimization_barrier((right, left, holds[count // 2]))
    far_a = shift(right[..., :half], axis, 1)
    far_b = shift(left[..., half:], axis, -1)
    pieces.append((jnp.concatenate([far_a, far_b], -1), (me + count // 2) % count))
    return pieces


def ring_sum(chunks, axis, holds):
    count = SIZES[axis]
    me = lax.axis_index(axis)
    far = chunks((me + count // 2) % count)
    half = far.shape[-1] // 2
    right = shift(far[..., :half].astype(BF), axis, 1)
    left = shift(far[..., half:].astype(BF), axis, -1)
    for step in range(count // 2 - 1, 0, -1):
        to_right = chunks((me + step) % count).astype(F32)
        to_left = chunks((me - step) % count).astype(F32)
        if step == count // 2 - 1:
            to_right = jnp.concatenate(
                [to_right[..., :half] + right.astype(F32), to_right[..., half:]], -1
            )
            to_left = jnp.concatenate(
                [to_left[..., :half], to_left[..., half:] + left.astype(F32)], -1
            )
        else:
            to_right = to_right + right.astype(F32)
            to_left = to_left + left.astype(F32)
        to_right, to_left = to_right.astype(BF), to_left.astype(BF)
        number = count // 2 - step + 1
        if number in holds:
            to_right, to_left, _ = lax.optimization_barrier((to_right, to_left, holds[number]))
        right = shift(to_right, axis, 1)
        left = shift(to_left, axis, -1)
    return chunks(me).astype(F32) + right.astype(F32) + left.astype(F32)


def near_x(own):
    return [own, shift(own, "x", 1), shift(own, "x", -1), shift(own, "x", 2)]


def scatter_near(parts):
    total = parts[0].astype(F32)
    for step, part in zip((-1, 1, 2), parts[1:]):
        total = total + shift(part, "x", step).astype(F32)
    return total


def scatter_grads(first, second):
    own, before, behind, far = (first[:, i] for i in range(4))
    half = far.shape[-1] // 2
    far_a = shift(far[..., :half], "x", 1)
    far_b = shift(far[..., half:], "x", -1)
    behind = jnp.concatenate([behind[..., :half].astype(F32) + far_a, behind[..., half:]], -1)
    before = jnp.concatenate([before[..., :half], before[..., half:].astype(F32) + far_b], -1)
    right = shift(behind.astype(BF), "x", 1)
    left = shift(before.astype(BF), "x", -1)
    by_x = (own.astype(F32) + right + left).astype(BF)
    holds = {2: (far_a, far_b), 4: by_x}
    by_z = ring_sum(lambda i: pick(second, i, 0), "z", holds).astype(BF)
    first = jnp.sum(lax.all_to_all(by_x, "z", 0, 0, tiled=True).astype(F32), 0)
    second = scatter_near([by_z[i] for i in range(4)])
    return jnp.concatenate([first, second], -1)


def dot(a, b, a_dim, b_dim):
    return lax.dot_general(a, b, (((a_dim,), (b_dim,)), ((), ())), preferred_element_type=F32)


def attend_block(own_ref, other_ref, own_map_ref, other_map_ref, load_ref, out_ref, mine_ref, theirs_ref):
    tokens = own_ref.shape[0]
    heads = out_ref.shape[1] // HD
    scale = HD ** (-0.5)
    own_map, other_map = own_map_ref[...], other_map_ref[...]
    keyval = (dot(own_ref[...], own_map, 1, 0) + dot(other_ref[...], other_map, 1, 0)).astype(BF)
    key, value = keyval[:, :HD], keyval[:, HD:]
    docs = load_ref[:, 2 * heads * HD :].astype(F32)
    row = lax.broadcasted_iota(jnp.int32, (tokens, tokens), 0)
    column = lax.broadcasted_iota(jnp.int32, (tokens, tokens), 1)
    allowed = (row // 8 == column // 8) & (column <= row) & (docs == docs.T)
    allowed = jnp.concatenate([allowed] * heads, 0)
    query, cot = (
        jnp.concatenate([load_ref[:, (n + i) * HD : (n + i + 1) * HD] for i in range(heads)], 0)
        for n in (0, heads)
    )
    scores = jnp.where(allowed, dot(query, key, 1, 1) * scale, -jnp.inf)
    prob_grad = dot(cot, value, 1, 1)
    exponent = jnp.exp(scores - jnp.max(scores, axis=1, keepdims=True))
    probs = exponent / jnp.sum(exponent, axis=1, keepdims=True)
    probs_bf = probs.astype(BF)
    score_grad = probs * (prob_grad - jnp.sum(probs * prob_grad, axis=1, keepdims=True))
    mixed = dot(probs_bf, value, 1, 0).astype(BF)
    for i in range(heads):
        out_ref[:, i * HD : (i + 1) * HD] = mixed[i * tokens : (i + 1) * tokens]
    key_grad = (dot(score_grad.astype(BF), query, 0, 0) * scale).astype(BF)
    value_grad = dot(probs_bf, cot, 0, 0).astype(BF)
    for ref, share in ((mine_ref, own_map), (theirs_ref, other_map)):
        ref[...] = (
            dot(key_grad, share[:, :HD], 1, 1) + dot(value_grad, share[:, HD:], 1, 1)
        ).astype(BF)


def attend(own, other, own_map, other_map, payload):
    rows, wide = payload.shape
    span = (wide - HD) // 2
    block = 128

    def rows_of(width):
        return pl.BlockSpec((block, width), lambda i: (i, 0))

    whole = pl.BlockSpec((HD, 2 * HD), lambda i: (0, 0))
    return pl.pallas_call(
        attend_block,
        grid=(rows // block,),
        in_specs=[rows_of(HD), rows_of(HD), whole, whole, rows_of(wide)],
        out_specs=[rows_of(span), rows_of(HD), rows_of(HD)],
        out_shape=[
            jax.ShapeDtypeStruct((rows, span), BF),
            jax.ShapeDtypeStruct((rows, HD), BF),
            jax.ShapeDtypeStruct((rows, HD), BF),
        ],
        cost_estimate=pl.CostEstimate(
            flops=12 * rows * block * span, bytes_accessed=4 * rows * wide, transcendentals=rows * span
        ),
    )(own, other, own_map, other_map, payload)


def column_map(core):
    share = lax.broadcasted_iota(jnp.int32, (HD, 2 * HD), 0)
    whole = lax.broadcasted_iota(jnp.int32, (HD, 2 * HD), 1)
    slot = share // 16 % 4
    offset = jnp.where(slot == 1, 3, jnp.where(slot == 2, 1, jnp.where(slot == 3, 2, 0)))
    x_index = (lax.axis_index("x") + offset) % 4
    target = share // 64 * HD + x_index * 32 + core * 16 + share % 16
    return (target == whole).astype(BF)


def body(hidden, assign, query, d_out, doc_ids, seq_len, w_kv):
    seqs, length, levels, features = hidden.shape
    width = levels * features
    rows = seqs * length
    core = lax.axis_index("c")
    head = lax.axis_index("y")
    live = (jnp.arange(length)[None, :] < seq_len[:, None])[:, :, None]
    zero = jnp.zeros((), BF)

    half = width // 2
    pairs = assign.reshape(-1, 2)
    order = jnp.where(core == 0, pairs, pairs[:, ::-1]).reshape(-1)
    with jax.named_scope("swap_rows"):
        slots = hidden.at[order].get(mode="promise_in_bounds").reshape(rows, width)
        both = jnp.concatenate([slots, shift(slots, "c", 1)], 0)
    with jax.named_scope("gather_w"):
        shard = w_kv.reshape(w_kv.shape[0], width)
        copies = jnp.broadcast_to(shard[None, :, :half], (8, shard.shape[0], half))
        by_z = lax.all_to_all(copies, "z", 0, 0, tiled=True)
        by_x = jnp.stack(near_x(shard[:, half:]))
        right, left = shift(by_z, "x", 1), shift(by_z, "x", -1)
        far_a = shift(right[..., : half // 2], "x", 1)
        far_b = shift(left[..., half // 2 :], "x", -1)
        first = jnp.stack([by_z, right, left, jnp.concatenate([far_a, far_b], -1)], 1)
        partial = dot(both[:, :half], first.reshape(-1, half), 1, 1)
        second = jnp.zeros((8,) + by_x.shape, BF)
        pieces = ring_gather(by_x, "z", {3: (right, left), 4: partial})
        for piece, index in pieces:
            second = place(second, piece[None], index)
    with jax.named_scope("send_queries"):
        docs = jnp.broadcast_to(doc_ids.astype(BF)[:, :, None], (seqs, length, HD))
        payload = jnp.concatenate([query, jnp.where(live, d_out, zero), docs], -1)
        payload = payload.reshape(seqs // 2, 2, length, -1)
        payload = jnp.stack([pick(payload, core, 1), shift(pick(payload, 1 - core, 1), "c", 1)], 1)
        payload = after(payload, pieces[-1][0], partial)
        payload = lax.all_to_all(payload, ("z", "x"), split_axis=0, concat_axis=0, tiled=True)
    with jax.named_scope("project"):
        partial = partial + dot(both[:, half:], second.reshape(-1, half), 1, 1)
    with jax.named_scope("sum_features"):
        def share(step):
            return lax.dynamic_slice(partial, (0, ((head + step) % 4) * HD), (2 * rows, HD))
        from_left = shift(share(1), "y", 1)
        from_right = shift(share(-1), "y", -1)
        from_far = shift(share(2), "y", 2)
        summed = (share(0) + from_left + from_right + from_far).astype(BF)
    with jax.named_scope("join_columns"):
        own_map, other_map = column_map(core), column_map(1 - core)
        other = shift(summed[rows:], "c", 1)
    with jax.named_scope("attention"):
        mixed_out, mine, theirs = attend(
            summed[:rows], other, own_map, other_map, payload.reshape(rows, -1)
        )
    with jax.named_scope("split_columns"):
        mine = jnp.concatenate([mine, shift(theirs, "c", 1)], 0)
    with jax.named_scope("gather_grads"):
        all_grads = jnp.zeros((2 * rows, 4 * HD), BF)
        for piece, step in (
            (mine, 0),
            (shift(mine, "y", 1), -1),
            (shift(mine, "y", -1), 1),
            (shift(mine, "y", 2), 2),
        ):
            all_grads = place(all_grads, piece, 0, ((head + step) % 4) * HD)
    with jax.named_scope("send_output"):
        mixed_out = mixed_out.reshape(seqs // 2, 2, length, -1)
        mixed_out = lax.all_to_all(mixed_out, ("z", "x"), split_axis=0, concat_axis=0, tiled=True)
        arrived, other = mixed_out[:, 0], shift(mixed_out[:, 1], "c", 1)
        mixed_out = jnp.where(
            core == 0, jnp.stack([arrived, other], 1), jnp.stack([other, arrived], 1)
        )
        mixed_out = jnp.where(live, mixed_out.reshape(query.shape), zero)
    with jax.named_scope("weight_grads"):
        first = dot(all_grads, both[:, :half], 0, 0).astype(BF)
        first = after(first, mixed_out)
        all_grads = after(all_grads, first)
        second = dot(all_grads, both[:, half:], 0, 0).astype(BF)
    with jax.named_scope("scatter_grads"):
        shape = (8, 4, w_kv.shape[0], half)
        grad_weight = scatter_grads(first.reshape(shape), second.reshape(shape))
    return mixed_out, grad_weight.reshape(w_kv.shape)


def solution(mesh):
    fine = Mesh(mesh.devices.reshape(8, 4, 2, 4), ("z", "x", "c", "y"))
    in_specs = (
        P(DP, None, None, "y"),
        P(DP),
        P(DP, None, "y"),
        P(DP, None, "y"),
        P(DP, None),
        P(DP),
        P(DP, None, "y"),
    )
    out_specs = (P(DP, None, "y"), P(DP, None, "y"))
    return jax.shard_map(body, mesh=fine, in_specs=in_specs, out_specs=out_specs, check_vma=False)
```

```python
import jax
import jax.numpy as jnp
from jax import lax
from jax.experimental import pallas as pl
from jax.experimental.pallas import tpu as pltpu
from jax.sharding import Mesh, PartitionSpec as P

HD = 128
BF = jnp.bfloat16
F32 = jnp.float32
SIZES = {"z": 8, "x": 4, "c": 2, "y": 4}
DP = ("z", "x", "c")


def shift(value, axis, step):
    count = SIZES[axis]
    return lax.ppermute(value, axis, [(i, (i + step) % count) for i in range(count)])


def place(buffer, piece, *index):
    index = index + (0,) * (buffer.ndim - len(index))
    return lax.dynamic_update_slice(buffer, piece, index)


def pick(stacked, index, dim=0):
    return lax.dynamic_index_in_dim(stacked, index, dim, keepdims=False)


def after(value, *others):
    return lax.optimization_barrier((value,) + others)[0]


def cut(width):
    return width // 2 // 128 * 128


def ring_gather(own, axis, holds):
    count = SIZES[axis]
    me = lax.axis_index(axis)
    half = cut(own.shape[-1])
    pieces = [(own, me)]
    right = left = own
    for step in range(1, count // 2):
        if step in holds:
            right, left, _ = lax.optimization_barrier((right, left, holds[step]))
        right = shift(right, axis, 1)
        left = shift(left, axis, -1)
        pieces.append((right, (me - step) % count))
        pieces.append((left, (me + step) % count))
    if count // 2 in holds:
        right, left, _ = lax.optimization_barrier((right, left, holds[count // 2]))
    far_a = shift(right[..., :half], axis, 1)
    far_b = shift(left[..., half:], axis, -1)
    pieces.append((jnp.concatenate([far_a, far_b], -1), (me + count // 2) % count))
    return pieces


def ring_sum(chunks, axis, holds):
    count = SIZES[axis]
    me = lax.axis_index(axis)
    far = chunks((me + count // 2) % count)
    half = cut(far.shape[-1])
    right = shift(far[..., :half].astype(BF), axis, 1)
    left = shift(far[..., half:].astype(BF), axis, -1)
    for step in range(count // 2 - 1, 0, -1):
        to_right = chunks((me + step) % count).astype(F32)
        to_left = chunks((me - step) % count).astype(F32)
        if step == count // 2 - 1:
            to_right = jnp.concatenate(
                [to_right[..., :half] + right.astype(F32), to_right[..., half:]], -1
            )
            to_left = jnp.concatenate(
                [to_left[..., :half], to_left[..., half:] + left.astype(F32)], -1
            )
        else:
            to_right = to_right + right.astype(F32)
            to_left = to_left + left.astype(F32)
        to_right, to_left = to_right.astype(BF), to_left.astype(BF)
        number = count // 2 - step + 1
        if number in holds:
            to_right, to_left, _ = lax.optimization_barrier((to_right, to_left, holds[number]))
        right = shift(to_right, axis, 1)
        left = shift(to_left, axis, -1)
    return chunks(me).astype(F32) + right.astype(F32) + left.astype(F32)


def near_x(own):
    return [own, shift(own, "x", 1), shift(own, "x", -1), shift(own, "x", 2)]


def scatter_near(parts):
    total = parts[0].astype(F32)
    for step, part in zip((-1, 1, 2), parts[1:]):
        total = total + shift(part, "x", step).astype(F32)
    return total


def scatter_grads(first, second):
    own, before, behind, far = (first[:, i] for i in range(4))
    half = cut(far.shape[-1])
    far_a = shift(far[..., :half], "x", 1)
    far_b = shift(far[..., half:], "x", -1)
    behind = jnp.concatenate([behind[..., :half].astype(F32) + far_a, behind[..., half:]], -1)
    before = jnp.concatenate([before[..., :half], before[..., half:].astype(F32) + far_b], -1)
    right = shift(behind.astype(BF), "x", 1)
    left = shift(before.astype(BF), "x", -1)
    by_x = (own.astype(F32) + right + left).astype(BF)
    holds = {2: (far_a, far_b), 4: by_x}
    by_z = ring_sum(lambda i: pick(second, i, 0), "z", holds).astype(BF)
    first = jnp.sum(lax.all_to_all(by_x, "z", 0, 0, tiled=True).astype(F32), 0)
    second = scatter_near([by_z[i] for i in range(4)])
    return jnp.concatenate([first, second], -1)


def dot(a, b, a_dim, b_dim):
    return lax.dot_general(a, b, (((a_dim,), (b_dim,)), ((), ())), preferred_element_type=F32)


def attend_block(place_ref, own_ref, other_ref, load_ref, out_ref, mine_ref, theirs_ref):
    tokens = own_ref.shape[0]
    heads = out_ref.shape[1] // HD
    scale = HD ** (-0.5)
    own_map, other_map = (column_map(place_ref[0], core) for core in (place_ref[1], 1 - place_ref[1]))
    keyval = (dot(own_ref[...], own_map, 1, 0) + dot(other_ref[...], other_map, 1, 0)).astype(BF)
    key, value = keyval[:, :HD], keyval[:, HD:]
    docs = load_ref[:, 2 * heads * HD :].astype(F32)
    row = lax.broadcasted_iota(jnp.int32, (tokens, tokens), 0)
    column = lax.broadcasted_iota(jnp.int32, (tokens, tokens), 1)
    allowed = (row // 8 == column // 8) & (column <= row) & (docs == docs.T)
    allowed = jnp.concatenate([allowed] * heads, 0)
    query, cot = (
        jnp.concatenate([load_ref[:, (n + i) * HD : (n + i + 1) * HD] for i in range(heads)], 0)
        for n in (0, heads)
    )
    scores = jnp.where(allowed, dot(query, key, 1, 1) * scale, -jnp.inf)
    prob_grad = dot(cot, value, 1, 1)
    exponent = jnp.exp(scores - jnp.max(scores, axis=1, keepdims=True))
    probs = exponent / jnp.sum(exponent, axis=1, keepdims=True)
    probs_bf = probs.astype(BF)
    score_grad = probs * (prob_grad - jnp.sum(probs * prob_grad, axis=1, keepdims=True))
    mixed = dot(probs_bf, value, 1, 0).astype(BF)
    for i in range(heads):
        out_ref[:, i * HD : (i + 1) * HD] = mixed[i * tokens : (i + 1) * tokens]
    key_grad = (dot(score_grad.astype(BF), query, 0, 0) * scale).astype(BF)
    value_grad = dot(probs_bf, cot, 0, 0).astype(BF)
    for ref, share in ((mine_ref, own_map), (theirs_ref, other_map)):
        ref[...] = (
            dot(key_grad, share[:, :HD], 1, 1) + dot(value_grad, share[:, HD:], 1, 1)
        ).astype(BF)


def attend(own, other, location, payload):
    rows, wide = payload.shape
    span = (wide - HD) // 2
    block = 128

    def rows_of(width):
        return pl.BlockSpec((block, width), lambda i: (i, 0))

    return pl.pallas_call(
        attend_block,
        grid=(rows // block,),
        in_specs=[pl.BlockSpec(memory_space=pltpu.SMEM), rows_of(HD), rows_of(HD), rows_of(wide)],
        out_specs=[rows_of(span), rows_of(HD), rows_of(HD)],
        out_shape=[
            jax.ShapeDtypeStruct((rows, span), BF),
            jax.ShapeDtypeStruct((rows, HD), BF),
            jax.ShapeDtypeStruct((rows, HD), BF),
        ],
        cost_estimate=pl.CostEstimate(
            flops=12 * rows * block * span, bytes_accessed=4 * rows * wide, transcendentals=rows * span
        ),
    )(location, own, other, payload)


def column_map(x_own, core):
    share = lax.broadcasted_iota(jnp.int32, (HD, 2 * HD), 0)
    whole = lax.broadcasted_iota(jnp.int32, (HD, 2 * HD), 1)
    slot = share // 16 % 4
    offset = jnp.where(slot == 1, 3, jnp.where(slot == 2, 1, jnp.where(slot == 3, 2, 0)))
    x_index = (x_own + offset) % 4
    target = share // 64 * HD + x_index * 32 + core * 16 + share % 16
    return (target == whole).astype(BF)


def body(hidden, assign, query, d_out, doc_ids, seq_len, w_kv):
    seqs, length, levels, features = hidden.shape
    width = levels * features
    rows = seqs * length
    core = lax.axis_index("c")
    head = lax.axis_index("y")
    live = (jnp.arange(length)[None, :] < seq_len[:, None])[:, :, None]
    zero = jnp.zeros((), BF)

    half = width // 2
    pairs = assign.reshape(-1, 2)
    order = jnp.where(core == 0, pairs, pairs[:, ::-1]).reshape(-1)
    with jax.named_scope("gather_w"):
        shard = w_kv.reshape(w_kv.shape[0], width)
        copies = jnp.broadcast_to(shard[None, :, :half], (8, shard.shape[0], half))
        by_z = lax.all_to_all(copies, "z", 0, 0, tiled=True)
        by_x = jnp.stack(near_x(shard[:, half:]))
    with jax.named_scope("swap_rows"):
        slots = hidden.at[after(order, by_x)].get(mode="promise_in_bounds").reshape(rows, width)
        both = jnp.concatenate([slots, shift(slots, "c", 1)], 0)
    with jax.named_scope("gather_w"):
        right, left = shift(by_z, "x", 1), shift(by_z, "x", -1)
        far_a = shift(right[..., : cut(half)], "x", 1)
        far_b = shift(left[..., cut(half) :], "x", -1)
        first = jnp.stack([by_z, right, left, jnp.concatenate([far_a, far_b], -1)], 1)
        partial = dot(both[:, :half], first.reshape(-1, half), 1, 1)
        second = jnp.zeros((8,) + by_x.shape, BF)
        pieces = ring_gather(by_x, "z", {2: by_z, 3: (right, left)})
        for piece, index in pieces:
            second = place(second, piece[None], index)
    with jax.named_scope("send_queries"):
        docs = jnp.broadcast_to(doc_ids.astype(BF)[:, :, None], (seqs, length, HD))
        payload = jnp.concatenate([query, jnp.where(live, d_out, zero), docs], -1)
        payload = payload.reshape(seqs // 2, 2, length, -1)
        payload = jnp.stack([pick(payload, core, 1), shift(pick(payload, 1 - core, 1), "c", 1)], 1)
        payload = after(payload, pieces[-1][0], partial)
        payload = lax.all_to_all(payload, ("z", "x"), split_axis=0, concat_axis=0, tiled=True)
    with jax.named_scope("project"):
        partial = partial + dot(both[:, half:], second.reshape(-1, half), 1, 1)
    with jax.named_scope("sum_features"):
        def share(step):
            return lax.dynamic_slice(partial, (0, ((head + step) % 4) * HD), (2 * rows, HD))
        from_left = shift(share(1), "y", 1)
        from_right = shift(share(-1), "y", -1)
        from_far = shift(share(2), "y", 2)
        summed = (share(0) + from_left + from_right + from_far).astype(BF)
    with jax.named_scope("join_columns"):
        location = jnp.stack([lax.axis_index("x"), core]).astype(jnp.int32)
        other = shift(summed[rows:], "c", 1)
    with jax.named_scope("attention"):
        mixed_out, mine, theirs = attend(
            summed[:rows], other, location, payload.reshape(rows, -1)
        )
    with jax.named_scope("split_columns"):
        mine = jnp.concatenate([mine, shift(theirs, "c", 1)], 0)
    with jax.named_scope("gather_grads"):
        all_grads = jnp.zeros((2 * rows, 4 * HD), BF)
        moved = [(mine, 0)] + [(shift(mine, "y", step), -step) for step in (1, -1, 2)]
        for piece, step in moved:
            all_grads = place(all_grads, piece, 0, ((head + step) % 4) * HD)
    with jax.named_scope("send_output"):
        mixed_out = mixed_out.reshape(seqs // 2, 2, length, -1)
        mixed_out = lax.all_to_all(mixed_out, ("z", "x"), split_axis=0, concat_axis=0, tiled=True)
        arrived, other = mixed_out[:, 0], shift(mixed_out[:, 1], "c", 1)
        mixed_out = jnp.where(
            core == 0, jnp.stack([arrived, other], 1), jnp.stack([other, arrived], 1)
        )
        mixed_out = jnp.where(live, mixed_out.reshape(query.shape), zero)
    with jax.named_scope("weight_grads"):
        first = dot(all_grads, both[:, :half], 0, 0).astype(BF)
        first = after(first, mixed_out)
        all_grads = after(all_grads, first)
        second = dot(all_grads, both[:, half:], 0, 0).astype(BF)
    with jax.named_scope("scatter_grads"):
        shape = (8, 4, w_kv.shape[0], half)
        grad_weight = scatter_grads(first.reshape(shape), second.reshape(shape))
    return mixed_out, grad_weight.reshape(w_kv.shape)


def solution(mesh):
    fine = Mesh(mesh.devices.reshape(8, 4, 2, 4), ("z", "x", "c", "y"))
    in_specs = (
        P(DP, None, None, "y"),
        P(DP),
        P(DP, None, "y"),
        P(DP, None, "y"),
        P(DP, None),
        P(DP),
        P(DP, None, "y"),
    )
    out_specs = (P(DP, None, "y"), P(DP, None, "y"))
    return jax.shard_map(body, mesh=fine, in_specs=in_specs, out_specs=out_specs, check_vma=False)
```

```python
import jax
import jax.numpy as jnp
from jax import lax
from jax.experimental import pallas as pl
from jax.experimental.pallas import tpu as pltpu
from jax.sharding import Mesh, PartitionSpec as P

HD = 128
BF = jnp.bfloat16
F32 = jnp.float32
SIZES = {"z": 8, "x": 4, "c": 2, "y": 4}
DP = ("z", "x", "c")


def shift(value, axis, step):
    count = SIZES[axis]
    return lax.ppermute(value, axis, [(i, (i + step) % count) for i in range(count)])


def place(buffer, piece, *index):
    index = index + (0,) * (buffer.ndim - len(index))
    return lax.dynamic_update_slice(buffer, piece, index)


def none_of(value):
    first = value[(0,) * value.ndim]
    return (first != first).astype(jnp.int32)


def pick(stacked, index, dim=0):
    return lax.dynamic_index_in_dim(stacked, index, dim, keepdims=False)


def after(value, *others):
    return lax.optimization_barrier((value,) + others)[0]


def cut(width):
    return width // 2 // 128 * 128


def ring_gather(own, axis, holds):
    count = SIZES[axis]
    me = lax.axis_index(axis)
    half = cut(own.shape[-1])
    pieces = [(own, me)]
    right = left = own
    for step in range(1, count // 2):
        if step in holds:
            right, left, _ = lax.optimization_barrier((right, left, holds[step]))
        right = shift(right, axis, 1)
        left = shift(left, axis, -1)
        pieces.append((right, (me - step) % count))
        pieces.append((left, (me + step) % count))
    if count // 2 in holds:
        right, left, _ = lax.optimization_barrier((right, left, holds[count // 2]))
    far_a = shift(right[..., :half], axis, 1)
    far_b = shift(left[..., half:], axis, -1)
    pieces.append((jnp.concatenate([far_a, far_b], -1), (me + count // 2) % count))
    return pieces


def ring_sum(chunks, axis, holds):
    count = SIZES[axis]
    me = lax.axis_index(axis)
    far = chunks((me + count // 2) % count)
    half = cut(far.shape[-1])
    right = shift(far[..., :half].astype(BF), axis, 1)
    left = shift(far[..., half:].astype(BF), axis, -1)
    for step in range(count // 2 - 1, 0, -1):
        number = count // 2 - step + 1
        wait = none_of(holds[number]) if number in holds else 0
        to_right = chunks((me + step + wait) % count).astype(F32)
        to_left = chunks((me - step + wait) % count).astype(F32)
        if step == count // 2 - 1:
            to_right = jnp.concatenate(
                [to_right[..., :half] + right.astype(F32), to_right[..., half:]], -1
            )
            to_left = jnp.concatenate(
                [to_left[..., :half], to_left[..., half:] + left.astype(F32)], -1
            )
        else:
            to_right = to_right + right.astype(F32)
            to_left = to_left + left.astype(F32)
        to_right, to_left = to_right.astype(BF), to_left.astype(BF)
        right = shift(to_right, axis, 1)
        left = shift(to_left, axis, -1)
    return chunks(me).astype(F32) + right.astype(F32) + left.astype(F32)


def near_x(own):
    return [own, shift(own, "x", 1), shift(own, "x", -1), shift(own, "x", 2)]


def scatter_near(parts):
    total = parts[0].astype(F32)
    for step, part in zip((-1, 1, 2), parts[1:]):
        total = total + shift(part, "x", step).astype(F32)
    return total


def scatter_grads(first, second):
    own, before, behind, far = (first[:, i] for i in range(4))
    half = cut(far.shape[-1])
    far_a = shift(far[..., :half], "x", 1)
    far_b = shift(far[..., half:], "x", -1)
    behind = jnp.concatenate([behind[..., :half].astype(F32) + far_a, behind[..., half:]], -1)
    before = jnp.concatenate([before[..., :half], before[..., half:].astype(F32) + far_b], -1)
    right = shift(behind.astype(BF), "x", 1)
    left = shift(before.astype(BF), "x", -1)
    by_x = (own.astype(F32) + right + left).astype(BF)
    holds = {4: by_x}
    by_z = ring_sum(lambda i: pick(second, i, 0), "z", holds).astype(BF)
    first = jnp.sum(lax.all_to_all(by_x, "z", 0, 0, tiled=True).astype(F32), 0)
    wait = none_of(first)
    second = scatter_near([pick(by_z, i + wait) for i in range(4)])
    return jnp.concatenate([first, second], -1)


def dot(a, b, a_dim, b_dim):
    return lax.dot_general(a, b, (((a_dim,), (b_dim,)), ((), ())), preferred_element_type=F32)


def attend_block(place_ref, own_ref, other_ref, load_ref, out_ref, mine_ref, theirs_ref):
    tokens = own_ref.shape[0]
    heads = out_ref.shape[1] // HD
    scale = HD ** (-0.5)
    own_map, other_map = (column_map(place_ref[0], core) for core in (place_ref[1], 1 - place_ref[1]))
    keyval = (dot(own_ref[...], own_map, 1, 0) + dot(other_ref[...], other_map, 1, 0)).astype(BF)
    key, value = keyval[:, :HD], keyval[:, HD:]
    docs = load_ref[:, 2 * heads * HD :].astype(F32)
    row = lax.broadcasted_iota(jnp.int32, (tokens, tokens), 0)
    column = lax.broadcasted_iota(jnp.int32, (tokens, tokens), 1)
    allowed = (row // 8 == column // 8) & (column <= row) & (docs == docs.T)
    allowed = jnp.concatenate([allowed] * heads, 0)
    query, cot = (
        jnp.concatenate([load_ref[:, (n + i) * HD : (n + i + 1) * HD] for i in range(heads)], 0)
        for n in (0, heads)
    )
    scores = jnp.where(allowed, dot(query, key, 1, 1) * scale, -jnp.inf)
    prob_grad = dot(cot, value, 1, 1)
    exponent = jnp.exp(scores - jnp.max(scores, axis=1, keepdims=True))
    probs = exponent / jnp.sum(exponent, axis=1, keepdims=True)
    probs_bf = probs.astype(BF)
    score_grad = probs * (prob_grad - jnp.sum(probs * prob_grad, axis=1, keepdims=True))
    mixed = dot(probs_bf, value, 1, 0).astype(BF)
    for i in range(heads):
        out_ref[:, i * HD : (i + 1) * HD] = mixed[i * tokens : (i + 1) * tokens]
    key_grad = (dot(score_grad.astype(BF), query, 0, 0) * scale).astype(BF)
    value_grad = dot(probs_bf, cot, 0, 0).astype(BF)
    for ref, share in ((mine_ref, own_map), (theirs_ref, other_map)):
        ref[...] = (
            dot(key_grad, share[:, :HD], 1, 1) + dot(value_grad, share[:, HD:], 1, 1)
        ).astype(BF)


def attend(own, other, location, payload):
    rows, wide = payload.shape
    span = (wide - HD) // 2
    block = 128

    def rows_of(width):
        return pl.BlockSpec((block, width), lambda i: (i, 0))

    return pl.pallas_call(
        attend_block,
        grid=(rows // block,),
        in_specs=[pl.BlockSpec(memory_space=pltpu.SMEM), rows_of(HD), rows_of(HD), rows_of(wide)],
        out_specs=[rows_of(span), rows_of(HD), rows_of(HD)],
        out_shape=[
            jax.ShapeDtypeStruct((rows, span), BF),
            jax.ShapeDtypeStruct((rows, HD), BF),
            jax.ShapeDtypeStruct((rows, HD), BF),
        ],
        cost_estimate=pl.CostEstimate(
            flops=12 * rows * block * span, bytes_accessed=4 * rows * wide, transcendentals=rows * span
        ),
    )(location, own, other, payload)


def column_map(x_own, core):
    share = lax.broadcasted_iota(jnp.int32, (HD, 2 * HD), 0)
    whole = lax.broadcasted_iota(jnp.int32, (HD, 2 * HD), 1)
    slot = share // 16 % 4
    offset = jnp.where(slot == 1, 3, jnp.where(slot == 2, 1, jnp.where(slot == 3, 2, 0)))
    x_index = (x_own + offset) % 4
    target = share // 64 * HD + x_index * 32 + core * 16 + share % 16
    return (target == whole).astype(BF)


def body(hidden, assign, query, d_out, doc_ids, seq_len, w_kv):
    seqs, length, levels, features = hidden.shape
    width = levels * features
    rows = seqs * length
    core = lax.axis_index("c")
    head = lax.axis_index("y")
    live = (jnp.arange(length)[None, :] < seq_len[:, None])[:, :, None]
    zero = jnp.zeros((), BF)

    half = width // 2
    pairs = assign.reshape(-1, 2)
    order = jnp.where(core == 0, pairs, pairs[:, ::-1]).reshape(-1)
    with jax.named_scope("gather_w"):
        shard = w_kv.reshape(w_kv.shape[0], width)
        copies = jnp.broadcast_to(shard[None, :, :half], (8, shard.shape[0], half))
        by_z = lax.all_to_all(copies, "z", 0, 0, tiled=True)
        by_x = jnp.stack(near_x(shard[:, half:]))
    with jax.named_scope("swap_rows"):
        slots = hidden.at[after(order, by_x)].get(mode="promise_in_bounds").reshape(rows, width)
        both = jnp.concatenate([slots, shift(slots, "c", 1)], 0)
    with jax.named_scope("gather_w"):
        right, left = shift(by_z, "x", 1), shift(by_z, "x", -1)
        far_a = shift(right[..., : cut(half)], "x", 1)
        far_b = shift(left[..., cut(half) :], "x", -1)
        first = jnp.stack([by_z, right, left, jnp.concatenate([far_a, far_b], -1)], 1)
        partial = dot(both[:, :half], first.reshape(-1, half), 1, 1)
        second = jnp.zeros((8,) + by_x.shape, BF)
        pieces = ring_gather(by_x, "z", {2: by_z, 3: (right, left)})
        for piece, index in pieces:
            second = place(second, piece[None], index)
    with jax.named_scope("send_queries"):
        docs = jnp.broadcast_to(doc_ids.astype(BF)[:, :, None], (seqs, length, HD))
        payload = jnp.concatenate([query, jnp.where(live, d_out, zero), docs], -1)
        payload = payload.reshape(seqs // 2, 2, length, -1)
        payload = jnp.stack([pick(payload, core, 1), shift(pick(payload, 1 - core, 1), "c", 1)], 1)
        payload = after(payload, pieces[-1][0], partial)
        payload = lax.all_to_all(payload, ("z", "x"), split_axis=0, concat_axis=0, tiled=True)
    with jax.named_scope("project"):
        partial = partial + dot(both[:, half:], second.reshape(-1, half), 1, 1)
    with jax.named_scope("sum_features"):
        def share(step):
            return lax.dynamic_slice(partial, (0, ((head + step) % 4) * HD), (2 * rows, HD))
        from_left = shift(share(1), "y", 1)
        from_right = shift(share(-1), "y", -1)
        from_far = shift(share(2), "y", 2)
        summed = (share(0) + from_left + from_right + from_far).astype(BF)
    with jax.named_scope("join_columns"):
        location = jnp.stack([lax.axis_index("x"), core]).astype(jnp.int32)
        other = shift(summed[rows:], "c", 1)
    with jax.named_scope("attention"):
        mixed_out, mine, theirs = attend(
            summed[:rows], other, location, payload.reshape(rows, -1)
        )
    with jax.named_scope("split_columns"):
        mine = jnp.concatenate([mine, shift(theirs, "c", 1)], 0)
    with jax.named_scope("gather_grads"):
        all_grads = jnp.zeros((2 * rows, 4 * HD), BF)
        moved = [(mine, 0)] + [(shift(mine, "y", step), -step) for step in (1, -1, 2)]
        for piece, step in moved:
            all_grads = place(all_grads, piece, 0, ((head + step) % 4) * HD)
    with jax.named_scope("send_output"):
        mixed_out = mixed_out.reshape(seqs // 2, 2, length, -1)
        mixed_out = lax.all_to_all(mixed_out, ("z", "x"), split_axis=0, concat_axis=0, tiled=True)
        arrived, other = mixed_out[:, 0], shift(mixed_out[:, 1], "c", 1)
        mixed_out = jnp.where(
            core == 0, jnp.stack([arrived, other], 1), jnp.stack([other, arrived], 1)
        )
        mixed_out = jnp.where(live, mixed_out.reshape(query.shape), zero)
    with jax.named_scope("weight_grads"):
        part = half
        first = dot(all_grads, both[:, :part], 0, 0).astype(BF)
        first = after(first, mixed_out)
        all_grads = after(all_grads, first)
        second = dot(all_grads, both[:, part:], 0, 0).astype(BF)
    with jax.named_scope("scatter_grads"):
        shape = (8, 4, w_kv.shape[0], -1)
        grad_weight = scatter_grads(first.reshape(shape), second.reshape(shape))
    return mixed_out, grad_weight.reshape(w_kv.shape)


def solution(mesh):
    fine = Mesh(mesh.devices.reshape(8, 4, 2, 4), ("z", "x", "c", "y"))
    in_specs = (
        P(DP, None, None, "y"),
        P(DP),
        P(DP, None, "y"),
        P(DP, None, "y"),
        P(DP, None),
        P(DP),
        P(DP, None, "y"),
    )
    out_specs = (P(DP, None, "y"), P(DP, None, "y"))
    return jax.shard_map(body, mesh=fine, in_specs=in_specs, out_specs=out_specs, check_vma=False)
```

```python
import jax
import jax.numpy as jnp
from jax import lax
from jax.experimental import pallas as pl
from jax.experimental.pallas import tpu as pltpu
from jax.sharding import Mesh, PartitionSpec as P

HD = 128
BF = jnp.bfloat16
F32 = jnp.float32
SIZES = {"z": 8, "x": 4, "c": 2, "y": 4}
DP = ("z", "x", "c")


def shift(value, axis, step):
    count = SIZES[axis]
    return lax.ppermute(value, axis, [(i, (i + step) % count) for i in range(count)])


def place(buffer, piece, *index):
    index = index + (0,) * (buffer.ndim - len(index))
    return lax.dynamic_update_slice(buffer, piece, index)


def none_of(*values):
    firsts = [value[(0,) * value.ndim] for value in values]
    return sum((first != first).astype(jnp.int32) for first in firsts)


def pick(stacked, index, dim=0):
    return lax.dynamic_index_in_dim(stacked, index, dim, keepdims=False)


def after(value, *others):
    return lax.optimization_barrier((value,) + others)[0]


def cut(width):
    return width // 2 // 128 * 128


def ring_gather(own, axis, holds):
    count = SIZES[axis]
    me = lax.axis_index(axis)
    half = cut(own.shape[-1])
    pieces = [(own, me)]
    right = left = own
    for step in range(1, count // 2):
        if step in holds:
            right, left, _ = lax.optimization_barrier((right, left, holds[step]))
        right = shift(right, axis, 1)
        left = shift(left, axis, -1)
        pieces.append((right, (me - step) % count))
        pieces.append((left, (me + step) % count))
    if count // 2 in holds:
        right, left, _ = lax.optimization_barrier((right, left, holds[count // 2]))
    far_a = shift(right[..., :half], axis, 1)
    far_b = shift(left[..., half:], axis, -1)
    pieces.append((jnp.concatenate([far_a, far_b], -1), (me + count // 2) % count))
    return pieces


def ring_sum(chunks, axis, holds):
    count = SIZES[axis]
    me = lax.axis_index(axis)
    wait = none_of(holds[1]) if 1 in holds else 0
    far = chunks((me + count // 2 + wait) % count)
    half = cut(far.shape[-1])
    right = shift(far[..., :half].astype(BF), axis, 1)
    left = shift(far[..., half:].astype(BF), axis, -1)
    for step in range(count // 2 - 1, 0, -1):
        to_right = chunks((me + step) % count).astype(F32)
        to_left = chunks((me - step) % count).astype(F32)
        if step == count // 2 - 1:
            to_right = jnp.concatenate(
                [to_right[..., :half] + right.astype(F32), to_right[..., half:]], -1
            )
            to_left = jnp.concatenate(
                [to_left[..., :half], to_left[..., half:] + left.astype(F32)], -1
            )
        else:
            to_right = to_right + right.astype(F32)
            to_left = to_left + left.astype(F32)
        to_right, to_left = to_right.astype(BF), to_left.astype(BF)
        number = count // 2 - step + 1
        if number in holds:
            to_right, to_left, _ = lax.optimization_barrier((to_right, to_left, holds[number]))
        right = shift(to_right, axis, 1)
        left = shift(to_left, axis, -1)
    return chunks(me).astype(F32) + right.astype(F32) + left.astype(F32)


def near_x(own):
    return [own, shift(own, "x", 1), shift(own, "x", -1), shift(own, "x", 2)]


def scatter_near(parts):
    total = parts[0].astype(F32)
    for step, part in zip((-1, 1, 2), parts[1:]):
        total = total + shift(part, "x", step).astype(F32)
    return total


def scatter_grads(first, second, hold):
    own, before, behind, far = (first[:, i] for i in range(4))
    half = cut(far.shape[-1])
    far_a = shift(far[..., :half], "x", 1)
    far_b = shift(far[..., half:], "x", -1)
    behind = jnp.concatenate([behind[..., :half].astype(F32) + far_a, behind[..., half:]], -1)
    before = jnp.concatenate([before[..., :half], before[..., half:].astype(F32) + far_b], -1)
    right = shift(behind.astype(BF), "x", 1)
    left = shift(before.astype(BF), "x", -1)
    by_x = (own.astype(F32) + right + left).astype(BF)
    holds = {1: hold, 2: (far_a, far_b), 4: by_x}
    by_z = ring_sum(lambda i: pick(second, i, 0), "z", holds).astype(BF)
    first = jnp.sum(lax.all_to_all(by_x, "z", 0, 0, tiled=True).astype(F32), 0)
    second = scatter_near([by_z[i] for i in range(4)])
    return jnp.concatenate([first, second], -1)


def dot(a, b, a_dim, b_dim):
    return lax.dot_general(a, b, (((a_dim,), (b_dim,)), ((), ())), preferred_element_type=F32)


def attend_block(place_ref, own_ref, other_ref, load_ref, out_ref, mine_ref, theirs_ref):
    tokens = own_ref.shape[0]
    heads = out_ref.shape[1] // HD
    scale = HD ** (-0.5)
    own_map, other_map = (column_map(place_ref[0], core) for core in (place_ref[1], 1 - place_ref[1]))
    keyval = (dot(own_ref[...], own_map, 1, 0) + dot(other_ref[...], other_map, 1, 0)).astype(BF)
    key, value = keyval[:, :HD], keyval[:, HD:]
    docs = load_ref[:, 2 * heads * HD :].astype(F32)
    row = lax.broadcasted_iota(jnp.int32, (tokens, tokens), 0)
    column = lax.broadcasted_iota(jnp.int32, (tokens, tokens), 1)
    allowed = (row // 8 == column // 8) & (column <= row) & (docs == docs.T)
    allowed = jnp.concatenate([allowed] * heads, 0)
    query, cot = (
        jnp.concatenate([load_ref[:, (n + i) * HD : (n + i + 1) * HD] for i in range(heads)], 0)
        for n in (0, heads)
    )
    scores = jnp.where(allowed, dot(query, key, 1, 1) * scale, -jnp.inf)
    prob_grad = dot(cot, value, 1, 1)
    exponent = jnp.exp(scores - jnp.max(scores, axis=1, keepdims=True))
    probs = exponent / jnp.sum(exponent, axis=1, keepdims=True)
    probs_bf = probs.astype(BF)
    score_grad = probs * (prob_grad - jnp.sum(probs * prob_grad, axis=1, keepdims=True))
    mixed = dot(probs_bf, value, 1, 0).astype(BF)
    for i in range(heads):
        out_ref[:, i * HD : (i + 1) * HD] = mixed[i * tokens : (i + 1) * tokens]
    key_grad = (dot(score_grad.astype(BF), query, 0, 0) * scale).astype(BF)
    value_grad = dot(probs_bf, cot, 0, 0).astype(BF)
    for ref, share in ((mine_ref, own_map), (theirs_ref, other_map)):
        ref[...] = (
            dot(key_grad, share[:, :HD], 1, 1) + dot(value_grad, share[:, HD:], 1, 1)
        ).astype(BF)


def attend(own, other, location, payload):
    rows, wide = payload.shape
    span = (wide - HD) // 2
    block = 128

    def rows_of(width):
        return pl.BlockSpec((block, width), lambda i: (i, 0))

    return pl.pallas_call(
        attend_block,
        grid=(rows // block,),
        in_specs=[pl.BlockSpec(memory_space=pltpu.SMEM), rows_of(HD), rows_of(HD), rows_of(wide)],
        out_specs=[rows_of(span), rows_of(HD), rows_of(HD)],
        out_shape=[
            jax.ShapeDtypeStruct((rows, span), BF),
            jax.ShapeDtypeStruct((rows, HD), BF),
            jax.ShapeDtypeStruct((rows, HD), BF),
        ],
        cost_estimate=pl.CostEstimate(
            flops=12 * rows * block * span, bytes_accessed=4 * rows * wide, transcendentals=rows * span
        ),
    )(location, own, other, payload)


def column_map(x_own, core):
    share = lax.broadcasted_iota(jnp.int32, (HD, 2 * HD), 0)
    whole = lax.broadcasted_iota(jnp.int32, (HD, 2 * HD), 1)
    slot = share // 16 % 4
    offset = jnp.where(slot == 1, 3, jnp.where(slot == 2, 1, jnp.where(slot == 3, 2, 0)))
    x_index = (x_own + offset) % 4
    target = share // 64 * HD + x_index * 32 + core * 16 + share % 16
    return (target == whole).astype(BF)


def body(hidden, assign, query, d_out, doc_ids, seq_len, w_kv):
    seqs, length, levels, features = hidden.shape
    width = levels * features
    rows = seqs * length
    core = lax.axis_index("c")
    head = lax.axis_index("y")
    live = (jnp.arange(length)[None, :] < seq_len[:, None])[:, :, None]
    zero = jnp.zeros((), BF)

    half = width // 2
    pairs = assign.reshape(-1, 2)
    order = jnp.where(core == 0, pairs, pairs[:, ::-1]).reshape(-1)
    with jax.named_scope("gather_w"):
        shard = w_kv.reshape(w_kv.shape[0], width)
        copies = jnp.broadcast_to(shard[None, :, :half], (8, shard.shape[0], half))
        by_z = lax.all_to_all(copies, "z", 0, 0, tiled=True)
        by_x = jnp.stack(near_x(shard[:, half:]))
    with jax.named_scope("swap_rows"):
        slots = hidden.at[after(order, by_x)].get(mode="promise_in_bounds").reshape(rows, width)
        both = jnp.concatenate([slots, shift(slots, "c", 1)], 0)
    with jax.named_scope("gather_w"):
        right, left = shift(by_z, "x", 1), shift(by_z, "x", -1)
        far_a = shift(right[..., : cut(half)], "x", 1)
        far_b = shift(left[..., cut(half) :], "x", -1)
        first = jnp.stack([by_z, right, left, jnp.concatenate([far_a, far_b], -1)], 1)
        partial = dot(both[:, :half], first.reshape(-1, half), 1, 1)
        second = jnp.zeros((8,) + by_x.shape, BF)
        pieces = ring_gather(by_x, "z", {2: by_z, 3: (right, left)})
        for piece, index in pieces:
            second = place(second, piece[None], index)
    with jax.named_scope("send_queries"):
        docs = jnp.broadcast_to(doc_ids.astype(BF)[:, :, None], (seqs, length, HD))
        payload = jnp.concatenate([query, jnp.where(live, d_out, zero), docs], -1)
        payload = payload.reshape(seqs // 2, 2, length, -1)
        payload = jnp.stack([pick(payload, core, 1), shift(pick(payload, 1 - core, 1), "c", 1)], 1)
        payload = after(payload, pieces[-1][0], partial)
        payload = lax.all_to_all(payload, ("z", "x"), split_axis=0, concat_axis=0, tiled=True)
    with jax.named_scope("project"):
        partial = partial + dot(both[:, half:], second.reshape(-1, half), 1, 1)
    with jax.named_scope("sum_features"):
        def share(step):
            return lax.dynamic_slice(partial, (0, ((head + step) % 4) * HD), (2 * rows, HD))
        from_left = shift(share(1), "y", 1)
        from_right = shift(share(-1), "y", -1)
        from_far = shift(share(2), "y", 2)
        summed = (share(0) + from_left + from_right + from_far).astype(BF)
    with jax.named_scope("join_columns"):
        location = jnp.stack([lax.axis_index("x"), core]).astype(jnp.int32)
        other = shift(summed[rows:], "c", 1)
    with jax.named_scope("attention"):
        mixed_out, mine, theirs = attend(
            summed[:rows], other, location, payload.reshape(rows, -1)
        )
    with jax.named_scope("split_columns"):
        mine = jnp.concatenate([mine, shift(theirs, "c", 1)], 0)
    with jax.named_scope("gather_grads"):
        all_grads = jnp.zeros((2 * rows, 4 * HD), BF)
        moved = [(mine, 0)] + [(shift(mine, "y", step), -step) for step in (1, -1, 2)]
        for piece, step in moved:
            all_grads = place(all_grads, piece, 0, ((head + step) % 4) * HD)
    with jax.named_scope("send_output"):
        wait = none_of(moved[2][0], moved[3][0]).astype(BF)
        mixed_out = (mixed_out + wait).reshape(seqs // 2, 2, length, -1)
        mixed_out = lax.all_to_all(mixed_out, ("z", "x"), split_axis=0, concat_axis=0, tiled=True)
        arrived, other = mixed_out[:, 0], shift(mixed_out[:, 1], "c", 1)
        mixed_out = jnp.where(
            core == 0, jnp.stack([arrived, other], 1), jnp.stack([other, arrived], 1)
        )
        mixed_out = jnp.where(live, mixed_out.reshape(query.shape), zero)
    with jax.named_scope("weight_grads"):
        first = dot(all_grads, both[:, :half], 0, 0).astype(BF)
        second = dot(after(all_grads, first), both[:, half:], 0, 0).astype(BF)
    with jax.named_scope("scatter_grads"):
        shape = (8, 4, w_kv.shape[0], half)
        grad_weight = scatter_grads(first.reshape(shape), second.reshape(shape), arrived)
    return mixed_out, grad_weight.reshape(w_kv.shape)


def solution(mesh):
    fine = Mesh(mesh.devices.reshape(8, 4, 2, 4), ("z", "x", "c", "y"))
    in_specs = (
        P(DP, None, None, "y"),
        P(DP),
        P(DP, None, "y"),
        P(DP, None, "y"),
        P(DP, None),
        P(DP),
        P(DP, None, "y"),
    )
    out_specs = (P(DP, None, "y"), P(DP, None, "y"))
    return jax.shard_map(body, mesh=fine, in_specs=in_specs, out_specs=out_specs, check_vma=False)
```

```python
import jax
import jax.numpy as jnp
from jax import lax
from jax.experimental import pallas as pl
from jax.experimental.pallas import tpu as pltpu
from jax.sharding import Mesh, PartitionSpec as P

HD = 128
BF = jnp.bfloat16
F32 = jnp.float32
SIZES = {"z": 8, "x": 4, "c": 2, "y": 4}
DP = ("z", "x", "c")


def shift(value, axis, step):
    count = SIZES[axis]
    return lax.ppermute(value, axis, [(i, (i + step) % count) for i in range(count)])


def place(buffer, piece, *index):
    index = index + (0,) * (buffer.ndim - len(index))
    return lax.dynamic_update_slice(buffer, piece, index)


def pick(stacked, index, dim=0):
    return lax.dynamic_index_in_dim(stacked, index, dim, keepdims=False)


def after(value, *others):
    return lax.optimization_barrier((value,) + others)[0]


def cut(width):
    return width // 2 // 128 * 128


def ring_gather(own, axis, holds):
    count = SIZES[axis]
    me = lax.axis_index(axis)
    half = cut(own.shape[-1])
    pieces = [(own, me)]
    right = left = own
    for step in range(1, count // 2):
        if step in holds:
            right, left, _ = lax.optimization_barrier((right, left, holds[step]))
        right = shift(right, axis, 1)
        left = shift(left, axis, -1)
        pieces.append((right, (me - step) % count))
        pieces.append((left, (me + step) % count))
    if count // 2 in holds:
        right, left, _ = lax.optimization_barrier((right, left, holds[count // 2]))
    far_a = shift(right[..., :half], axis, 1)
    far_b = shift(left[..., half:], axis, -1)
    pieces.append((jnp.concatenate([far_a, far_b], -1), (me + count // 2) % count))
    return pieces


def ring_sum(chunks, axis, holds):
    count = SIZES[axis]
    me = lax.axis_index(axis)
    far = chunks((me + count // 2) % count)
    half = cut(far.shape[-1])
    right = shift(far[..., :half].astype(BF), axis, 1)
    left = shift(far[..., half:].astype(BF), axis, -1)
    for step in range(count // 2 - 1, 0, -1):
        to_right = chunks((me + step) % count).astype(F32)
        to_left = chunks((me - step) % count).astype(F32)
        if step == count // 2 - 1:
            to_right = jnp.concatenate(
                [to_right[..., :half] + right.astype(F32), to_right[..., half:]], -1
            )
            to_left = jnp.concatenate(
                [to_left[..., :half], to_left[..., half:] + left.astype(F32)], -1
            )
        else:
            to_right = to_right + right.astype(F32)
            to_left = to_left + left.astype(F32)
        to_right, to_left = to_right.astype(BF), to_left.astype(BF)
        number = count // 2 - step + 1
        if number in holds:
            to_right, to_left, _ = lax.optimization_barrier((to_right, to_left, holds[number]))
        right = shift(to_right, axis, 1)
        left = shift(to_left, axis, -1)
    return chunks(me).astype(F32) + right.astype(F32) + left.astype(F32)


def near_x(own):
    return [own, shift(own, "x", 1), shift(own, "x", -1), shift(own, "x", 2)]


def scatter_near(parts):
    total = parts[0].astype(F32)
    for step, part in zip((-1, 1, 2), parts[1:]):
        total = total + shift(part, "x", step).astype(F32)
    return total


def scatter_grads(first, second):
    own, before, behind, far = (first[:, i] for i in range(4))
    half = cut(far.shape[-1])
    far_a = shift(far[..., :half], "x", 1)
    far_b = shift(far[..., half:], "x", -1)
    behind = jnp.concatenate([behind[..., :half].astype(F32) + far_a, behind[..., half:]], -1)
    before = jnp.concatenate([before[..., :half], before[..., half:].astype(F32) + far_b], -1)
    right = shift(behind.astype(BF), "x", 1)
    left = shift(before.astype(BF), "x", -1)
    by_x = (own.astype(F32) + right + left).astype(BF)
    holds = {2: (far_a, far_b), 4: by_x}
    by_z = ring_sum(lambda i: pick(second, i, 0), "z", holds).astype(BF)
    first = jnp.sum(lax.all_to_all(by_x, "z", 0, 0, tiled=True).astype(F32), 0)
    second = scatter_near([by_z[i] for i in range(4)])
    return jnp.concatenate([first, second], -1)


def dot(a, b, a_dim, b_dim):
    return lax.dot_general(a, b, (((a_dim,), (b_dim,)), ((), ())), preferred_element_type=F32)


def attend_block(place_ref, own_ref, other_ref, load_ref, out_ref, mine_ref, theirs_ref):
    tokens = own_ref.shape[0]
    heads = out_ref.shape[1] // HD
    scale = HD ** (-0.5)
    own_map, other_map = (column_map(place_ref[0], core) for core in (place_ref[1], 1 - place_ref[1]))
    keyval = (dot(own_ref[...], own_map, 1, 0) + dot(other_ref[...], other_map, 1, 0)).astype(BF)
    key, value = keyval[:, :HD], keyval[:, HD:]
    docs = load_ref[:, 2 * heads * HD :].astype(F32)
    row = lax.broadcasted_iota(jnp.int32, (tokens, tokens), 0)
    column = lax.broadcasted_iota(jnp.int32, (tokens, tokens), 1)
    allowed = (row // 8 == column // 8) & (column <= row) & (docs == docs.T)
    allowed = jnp.concatenate([allowed] * heads, 0)
    query, cot = (
        jnp.concatenate([load_ref[:, (n + i) * HD : (n + i + 1) * HD] for i in range(heads)], 0)
        for n in (0, heads)
    )
    scores = jnp.where(allowed, dot(query, key, 1, 1) * scale, -jnp.inf)
    prob_grad = dot(cot, value, 1, 1)
    exponent = jnp.exp(scores - jnp.max(scores, axis=1, keepdims=True))
    probs = exponent / jnp.sum(exponent, axis=1, keepdims=True)
    probs_bf = probs.astype(BF)
    score_grad = probs * (prob_grad - jnp.sum(probs * prob_grad, axis=1, keepdims=True))
    mixed = dot(probs_bf, value, 1, 0).astype(BF)
    for i in range(heads):
        out_ref[:, i * HD : (i + 1) * HD] = mixed[i * tokens : (i + 1) * tokens]
    key_grad = (dot(score_grad.astype(BF), query, 0, 0) * scale).astype(BF)
    value_grad = dot(probs_bf, cot, 0, 0).astype(BF)
    for ref, share in ((mine_ref, own_map), (theirs_ref, other_map)):
        ref[...] = (
            dot(key_grad, share[:, :HD], 1, 1) + dot(value_grad, share[:, HD:], 1, 1)
        ).astype(BF)


def attend(own, other, location, payload):
    rows, wide = payload.shape
    span = (wide - HD) // 2
    block = 128

    def rows_of(width):
        return pl.BlockSpec((block, width), lambda i: (i, 0))

    return pl.pallas_call(
        attend_block,
        grid=(rows // block,),
        in_specs=[pl.BlockSpec(memory_space=pltpu.SMEM), rows_of(HD), rows_of(HD), rows_of(wide)],
        out_specs=[rows_of(span), rows_of(HD), rows_of(HD)],
        out_shape=[
            jax.ShapeDtypeStruct((rows, span), BF),
            jax.ShapeDtypeStruct((rows, HD), BF),
            jax.ShapeDtypeStruct((rows, HD), BF),
        ],
        cost_estimate=pl.CostEstimate(
            flops=12 * rows * block * span, bytes_accessed=4 * rows * wide, transcendentals=rows * span
        ),
    )(location, own, other, payload)


def column_map(x_own, core):
    share = lax.broadcasted_iota(jnp.int32, (HD, 2 * HD), 0)
    whole = lax.broadcasted_iota(jnp.int32, (HD, 2 * HD), 1)
    slot = share // 16 % 4
    offset = jnp.where(slot == 1, 3, jnp.where(slot == 2, 1, jnp.where(slot == 3, 2, 0)))
    x_index = (x_own + offset) % 4
    target = share // 64 * HD + x_index * 32 + core * 16 + share % 16
    return (target == whole).astype(BF)


def body(hidden, assign, query, d_out, doc_ids, seq_len, w_kv):
    seqs, length, levels, features = hidden.shape
    width = levels * features
    rows = seqs * length
    core = lax.axis_index("c")
    head = lax.axis_index("y")
    live = (jnp.arange(length)[None, :] < seq_len[:, None])[:, :, None]
    zero = jnp.zeros((), BF)

    half = width // 2
    pairs = assign.reshape(-1, 2)
    order = jnp.where(core == 0, pairs, pairs[:, ::-1]).reshape(-1)
    with jax.named_scope("gather_w"):
        shard = w_kv.reshape(w_kv.shape[0], width)
        copies = jnp.broadcast_to(shard[None, :, :half], (8, shard.shape[0], half))
        by_z = lax.all_to_all(copies, "z", 0, 0, tiled=True)
        by_x = jnp.stack(near_x(shard[:, half:]))
    with jax.named_scope("swap_rows"):
        slots = hidden.at[after(order, by_x)].get(mode="promise_in_bounds").reshape(rows, width)
        both = jnp.concatenate([slots, shift(slots, "c", 1)], 0)
    with jax.named_scope("gather_w"):
        shares = near_x(by_z)
        first = jnp.stack(shares, 1)
        partial = dot(both[:, :half], first.reshape(-1, half), 1, 1)
        second = jnp.zeros((8,) + by_x.shape, BF)
        pieces = ring_gather(by_x, "z", {2: by_z})
        for piece, index in pieces:
            second = place(second, piece[None], index)
    with jax.named_scope("send_queries"):
        docs = jnp.broadcast_to(doc_ids.astype(BF)[:, :, None], (seqs, length, HD))
        payload = jnp.concatenate([query, jnp.where(live, d_out, zero), docs], -1)
        payload = payload.reshape(seqs // 2, 2, length, -1)
        payload = jnp.stack([pick(payload, core, 1), shift(pick(payload, 1 - core, 1), "c", 1)], 1)
        payload = after(payload, pieces[-1][0], partial)
        payload = lax.all_to_all(payload, ("z", "x"), split_axis=0, concat_axis=0, tiled=True)
    with jax.named_scope("project"):
        partial = partial + dot(both[:, half:], second.reshape(-1, half), 1, 1)
    with jax.named_scope("sum_features"):
        def share(step):
            return lax.dynamic_slice(partial, (0, ((head + step) % 4) * HD), (2 * rows, HD))
        from_left = shift(share(1), "y", 1)
        from_right = shift(share(-1), "y", -1)
        from_far = shift(share(2), "y", 2)
        summed = (share(0) + from_left + from_right + from_far).astype(BF)
    with jax.named_scope("join_columns"):
        location = jnp.stack([lax.axis_index("x"), core]).astype(jnp.int32)
        other = shift(summed[rows:], "c", 1)
    with jax.named_scope("attention"):
        mixed_out, mine, theirs = attend(
            summed[:rows], other, location, payload.reshape(rows, -1)
        )
    with jax.named_scope("split_columns"):
        mine = jnp.concatenate([mine, shift(theirs, "c", 1)], 0)
    with jax.named_scope("gather_grads"):
        all_grads = jnp.zeros((2 * rows, 4 * HD), BF)
        moved = [(mine, 0)] + [(shift(mine, "y", step), -step) for step in (1, -1, 2)]
        for piece, step in moved:
            all_grads = place(all_grads, piece, 0, ((head + step) % 4) * HD)
    with jax.named_scope("send_output"):
        mixed_out = mixed_out.reshape(seqs // 2, 2, length, -1)
        mixed_out = lax.all_to_all(mixed_out, ("z", "x"), split_axis=0, concat_axis=0, tiled=True)
        arrived, other = mixed_out[:, 0], shift(mixed_out[:, 1], "c", 1)
        mixed_out = jnp.where(
            core == 0, jnp.stack([arrived, other], 1), jnp.stack([other, arrived], 1)
        )
        mixed_out = jnp.where(live, mixed_out.reshape(query.shape), zero)
    with jax.named_scope("weight_grads"):
        first = dot(all_grads, both[:, :half], 0, 0).astype(BF)
        first = after(first, mixed_out)
        all_grads = after(all_grads, first)
        second = dot(all_grads, both[:, half:], 0, 0).astype(BF)
    with jax.named_scope("scatter_grads"):
        shape = (8, 4, w_kv.shape[0], half)
        grad_weight = scatter_grads(first.reshape(shape), second.reshape(shape))
    return mixed_out, grad_weight.reshape(w_kv.shape)


def solution(mesh):
    fine = Mesh(mesh.devices.reshape(8, 4, 2, 4), ("z", "x", "c", "y"))
    in_specs = (
        P(DP, None, None, "y"),
        P(DP),
        P(DP, None, "y"),
        P(DP, None, "y"),
        P(DP, None),
        P(DP),
        P(DP, None, "y"),
    )
    out_specs = (P(DP, None, "y"), P(DP, None, "y"))
    return jax.shard_map(body, mesh=fine, in_specs=in_specs, out_specs=out_specs, check_vma=False)
```

```python
import jax
import jax.numpy as jnp
from jax import lax
from jax.experimental import pallas as pl
from jax.experimental.pallas import tpu as pltpu
from jax.sharding import Mesh, PartitionSpec as P

HD = 128
BF = jnp.bfloat16
F32 = jnp.float32
SIZES = {"z": 8, "x": 4, "c": 2, "y": 4}
DP = ("z", "x", "c")


def shift(value, axis, step):
    count = SIZES[axis]
    return lax.ppermute(value, axis, [(i, (i + step) % count) for i in range(count)])


def place(buffer, piece, *index):
    index = index + (0,) * (buffer.ndim - len(index))
    return lax.dynamic_update_slice(buffer, piece, index)


def pick(stacked, index, dim=0):
    return lax.dynamic_index_in_dim(stacked, index, dim, keepdims=False)


def after(value, *others):
    return lax.optimization_barrier((value,) + others)[0]


def cut(width):
    return width // 2 // 128 * 128


def ring_gather(own, axis, holds):
    count = SIZES[axis]
    me = lax.axis_index(axis)
    half = cut(own.shape[-1])
    pieces = [(own, me)]
    right = left = own
    for step in range(1, count // 2):
        if step in holds:
            right, left, _ = lax.optimization_barrier((right, left, holds[step]))
        right = shift(right, axis, 1)
        left = shift(left, axis, -1)
        pieces.append((right, (me - step) % count))
        pieces.append((left, (me + step) % count))
    if count // 2 in holds:
        right, left, _ = lax.optimization_barrier((right, left, holds[count // 2]))
    far_a = shift(right[..., :half], axis, 1)
    far_b = shift(left[..., half:], axis, -1)
    pieces.append((jnp.concatenate([far_a, far_b], -1), (me + count // 2) % count))
    return pieces


def ring_sum(chunks, axis, holds):
    count = SIZES[axis]
    me = lax.axis_index(axis)
    far = chunks((me + count // 2) % count)
    half = cut(far.shape[-1])
    right = shift(far[..., :half].astype(BF), axis, 1)
    left = shift(far[..., half:].astype(BF), axis, -1)
    for step in range(count // 2 - 1, 0, -1):
        to_right = chunks((me + step) % count).astype(F32)
        to_left = chunks((me - step) % count).astype(F32)
        if step == count // 2 - 1:
            to_right = jnp.concatenate(
                [to_right[..., :half] + right.astype(F32), to_right[..., half:]], -1
            )
            to_left = jnp.concatenate(
                [to_left[..., :half], to_left[..., half:] + left.astype(F32)], -1
            )
        else:
            to_right = to_right + right.astype(F32)
            to_left = to_left + left.astype(F32)
        to_right, to_left = to_right.astype(BF), to_left.astype(BF)
        number = count // 2 - step + 1
        if number in holds:
            to_right, to_left, _ = lax.optimization_barrier((to_right, to_left, holds[number]))
        right = shift(to_right, axis, 1)
        left = shift(to_left, axis, -1)
    return chunks(me).astype(F32) + right.astype(F32) + left.astype(F32)


def near_x(own):
    return [own, shift(own, "x", 1), shift(own, "x", -1), shift(own, "x", 2)]


def scatter_near(parts):
    total = parts[0].astype(F32)
    for step, part in zip((-1, 1, 2), parts[1:]):
        total = total + shift(part, "x", step).astype(F32)
    return total


def scatter_grads(first, second):
    own, before, behind, far = (first[:, i] for i in range(4))
    half = cut(far.shape[-1])
    far_a = shift(far[..., :half], "x", 1)
    far_b = shift(far[..., half:], "x", -1)
    behind = jnp.concatenate([behind[..., :half].astype(F32) + far_a, behind[..., half:]], -1)
    before = jnp.concatenate([before[..., :half], before[..., half:].astype(F32) + far_b], -1)
    right = shift(behind.astype(BF), "x", 1)
    left = shift(before.astype(BF), "x", -1)
    by_x = (own.astype(F32) + right + left).astype(BF)
    holds = {2: (far_a, far_b), 4: by_x}
    by_z = ring_sum(lambda i: pick(second, i, 0), "z", holds).astype(BF)
    first = jnp.sum(lax.all_to_all(by_x, "z", 0, 0, tiled=True).astype(F32), 0)
    second = scatter_near([by_z[i] for i in range(4)])
    return jnp.concatenate([first, second], -1)


def dot(a, b, a_dim, b_dim):
    return lax.dot_general(a, b, (((a_dim,), (b_dim,)), ((), ())), preferred_element_type=F32)


def attend_block(place_ref, own_ref, other_ref, load_ref, out_ref, mine_ref, theirs_ref):
    tokens = own_ref.shape[0]
    heads = out_ref.shape[1] // HD
    scale = HD ** (-0.5)
    own_map, other_map = (column_map(place_ref[0], core) for core in (place_ref[1], 1 - place_ref[1]))
    keyval = (dot(own_ref[...], own_map, 1, 0) + dot(other_ref[...], other_map, 1, 0)).astype(BF)
    key, value = keyval[:, :HD], keyval[:, HD:]
    docs = load_ref[:, 2 * heads * HD :].astype(F32)
    row = lax.broadcasted_iota(jnp.int32, (tokens, tokens), 0)
    column = lax.broadcasted_iota(jnp.int32, (tokens, tokens), 1)
    allowed = (row // 8 == column // 8) & (column <= row) & (docs == docs.T)
    allowed = jnp.concatenate([allowed] * heads, 0)
    query, cot = (
        jnp.concatenate([load_ref[:, (n + i) * HD : (n + i + 1) * HD] for i in range(heads)], 0)
        for n in (0, heads)
    )
    scores = jnp.where(allowed, dot(query, key, 1, 1) * scale, -jnp.inf)
    prob_grad = dot(cot, value, 1, 1)
    exponent = jnp.exp(scores - jnp.max(scores, axis=1, keepdims=True))
    probs = exponent / jnp.sum(exponent, axis=1, keepdims=True)
    probs_bf = probs.astype(BF)
    score_grad = probs * (prob_grad - jnp.sum(probs * prob_grad, axis=1, keepdims=True))
    mixed = dot(probs_bf, value, 1, 0).astype(BF)
    for i in range(heads):
        out_ref[:, i * HD : (i + 1) * HD] = mixed[i * tokens : (i + 1) * tokens]
    key_grad = (dot(score_grad.astype(BF), query, 0, 0) * scale).astype(BF)
    value_grad = dot(probs_bf, cot, 0, 0).astype(BF)
    for ref, share in ((mine_ref, own_map), (theirs_ref, other_map)):
        ref[...] = (
            dot(key_grad, share[:, :HD], 1, 1) + dot(value_grad, share[:, HD:], 1, 1)
        ).astype(BF)


def attend(own, other, location, payload):
    rows, wide = payload.shape
    span = (wide - HD) // 2
    block = 128

    def rows_of(width):
        return pl.BlockSpec((block, width), lambda i: (i, 0))

    return pl.pallas_call(
        attend_block,
        grid=(rows // block,),
        in_specs=[pl.BlockSpec(memory_space=pltpu.SMEM), rows_of(HD), rows_of(HD), rows_of(wide)],
        out_specs=[rows_of(span), rows_of(HD), rows_of(HD)],
        out_shape=[
            jax.ShapeDtypeStruct((rows, span), BF),
            jax.ShapeDtypeStruct((rows, HD), BF),
            jax.ShapeDtypeStruct((rows, HD), BF),
        ],
        cost_estimate=pl.CostEstimate(
            flops=12 * rows * block * span, bytes_accessed=4 * rows * wide, transcendentals=rows * span
        ),
    )(location, own, other, payload)


def column_map(x_own, core):
    share = lax.broadcasted_iota(jnp.int32, (HD, 2 * HD), 0)
    whole = lax.broadcasted_iota(jnp.int32, (HD, 2 * HD), 1)
    slot = share // 16 % 4
    offset = jnp.where(slot == 1, 3, jnp.where(slot == 2, 1, jnp.where(slot == 3, 2, 0)))
    x_index = (x_own + offset) % 4
    target = share // 64 * HD + x_index * 32 + core * 16 + share % 16
    return (target == whole).astype(BF)


def body(hidden, assign, query, d_out, doc_ids, seq_len, w_kv):
    seqs, length, levels, features = hidden.shape
    width = levels * features
    rows = seqs * length
    core = lax.axis_index("c")
    head = lax.axis_index("y")
    live = (jnp.arange(length)[None, :] < seq_len[:, None])[:, :, None]
    zero = jnp.zeros((), BF)

    half = width // 2
    pairs = assign.reshape(-1, 2)
    order = jnp.where(core == 0, pairs, pairs[:, ::-1]).reshape(-1)
    with jax.named_scope("gather_w"):
        shard = w_kv.reshape(w_kv.shape[0], width)
        copies = jnp.broadcast_to(shard[None, :, :half], (8, shard.shape[0], half))
        by_z = lax.all_to_all(copies, "z", 0, 0, tiled=True)
        by_x = jnp.stack(near_x(shard[:, half:]))
    with jax.named_scope("swap_rows"):
        slots = hidden.at[after(order, by_x)].get(mode="promise_in_bounds").reshape(rows, width)
        both = jnp.concatenate([slots, shift(slots, "c", 1)], 0)
    with jax.named_scope("gather_w"):
        shares = near_x(by_z)
        weights = jnp.zeros((8,) + by_x.shape[:2] + (width,), BF)
        for i, share in enumerate(shares):
            weights = place(weights, share[:, None], 0, i)
        pieces = ring_gather(by_x, "z", {2: by_z})
        for piece, index in pieces:
            weights = place(weights, piece[None], index, 0, 0, half)
    with jax.named_scope("send_queries"):
        docs = jnp.broadcast_to(doc_ids.astype(BF)[:, :, None], (seqs, length, HD))
        payload = jnp.concatenate([query, jnp.where(live, d_out, zero), docs], -1)
        payload = payload.reshape(seqs // 2, 2, length, -1)
        payload = jnp.stack([pick(payload, core, 1), shift(pick(payload, 1 - core, 1), "c", 1)], 1)
        payload = after(payload, pieces[-1][0], shares)
        payload = lax.all_to_all(payload, ("z", "x"), split_axis=0, concat_axis=0, tiled=True)
    with jax.named_scope("project"):
        partial = dot(both, weights.reshape(-1, width), 1, 1)
    with jax.named_scope("sum_features"):
        def share(step):
            return lax.dynamic_slice(partial, (0, ((head + step) % 4) * HD), (2 * rows, HD))
        from_left = shift(share(1), "y", 1)
        from_right = shift(share(-1), "y", -1)
        from_far = shift(share(2), "y", 2)
        summed = (share(0) + from_left + from_right + from_far).astype(BF)
    with jax.named_scope("join_columns"):
        location = jnp.stack([lax.axis_index("x"), core]).astype(jnp.int32)
        other = shift(summed[rows:], "c", 1)
    with jax.named_scope("attention"):
        mixed_out, mine, theirs = attend(
            summed[:rows], other, location, payload.reshape(rows, -1)
        )
    with jax.named_scope("split_columns"):
        mine = jnp.concatenate([mine, shift(theirs, "c", 1)], 0)
    with jax.named_scope("gather_grads"):
        all_grads = jnp.zeros((2 * rows, 4 * HD), BF)
        moved = [(mine, 0)] + [(shift(mine, "y", step), -step) for step in (1, -1, 2)]
        for piece, step in moved:
            all_grads = place(all_grads, piece, 0, ((head + step) % 4) * HD)
    with jax.named_scope("send_output"):
        mixed_out = mixed_out.reshape(seqs // 2, 2, length, -1)
        mixed_out = lax.all_to_all(mixed_out, ("z", "x"), split_axis=0, concat_axis=0, tiled=True)
        arrived, other = mixed_out[:, 0], shift(mixed_out[:, 1], "c", 1)
        mixed_out = jnp.where(
            core == 0, jnp.stack([arrived, other], 1), jnp.stack([other, arrived], 1)
        )
        mixed_out = jnp.where(live, mixed_out.reshape(query.shape), zero)
    with jax.named_scope("weight_grads"):
        first = dot(all_grads, both[:, :half], 0, 0).astype(BF)
        first = after(first, mixed_out)
        all_grads = after(all_grads, first)
        second = dot(all_grads, both[:, half:], 0, 0).astype(BF)
    with jax.named_scope("scatter_grads"):
        shape = (8, 4, w_kv.shape[0], half)
        grad_weight = scatter_grads(first.reshape(shape), second.reshape(shape))
    return mixed_out, grad_weight.reshape(w_kv.shape)


def solution(mesh):
    fine = Mesh(mesh.devices.reshape(8, 4, 2, 4), ("z", "x", "c", "y"))
    in_specs = (
        P(DP, None, None, "y"),
        P(DP),
        P(DP, None, "y"),
        P(DP, None, "y"),
        P(DP, None),
        P(DP),
        P(DP, None, "y"),
    )
    out_specs = (P(DP, None, "y"), P(DP, None, "y"))
    return jax.shard_map(body, mesh=fine, in_specs=in_specs, out_specs=out_specs, check_vma=False)
```
